32 devices in a mesh: groups: 1, seq: 8 (over z, y), chan: 2 (over x), sub: 2 (over core).
Axes of the slice: x: 2, y: 2, z: 4, core: 2. Of those that a mesh axis runs over, the one named last changes fastest.
Arguments:
- projections: bfloat16 [3, 256, 131072], P(None, 'chan', ('groups', 'seq', 'sub')), may hold values from -6 to 6
- short_taps: float32 [3, 3, 256], P(None, None, 'chan'), may hold values from -4 to 4
- skip_gain: float32 [256], P('chan'), may hold values from -5 to 5
- filter_spec: bfloat16 [2, 256, 8, 7168], P(None, ('chan', 'seq', 'sub')), may hold values from -18 to 18
- keep_first: int32 [64], replicated, may hold values from 0 to 127, as said below
- keep_second: int32 [112], replicated, may hold values from 0 to 127, as said below
- keep_third: int32 [8], replicated, may hold values from 0 to 15, as said below
- out_weight: bfloat16 [256, 256], P(None, 'chan'), may hold values from -0.375 to 0.375
Outputs:
- mixed_out: bfloat16 [256, 131072], P('chan', ('groups', 'seq', 'sub'))
The draws below stay inside these ranges and needn't reach their ends.
Inputs may be any that keep to these rules, and one draw needn't show every extreme that they name: `keep_first`: distinct and increasing, always holding 0 and 127. `keep_second`: distinct and increasing, always holding 0 and 127. `keep_third`: distinct and increasing, always holding 0 and 15.
All inputs are finite; a program needn't handle non-finite values.
Results may differ from the reference program's by a relative error of at most 0.011.
Values may be sent and summed in bfloat16 or wider, within the bound.
A program may use at most 128 MiB of HBM per device.

```python
import math
import jax
import jax.numpy as jnp
from jax import lax

D = 256
TOKENS = 131072
A = 128
B = 128
C = 16
K1 = 64
K2 = 112
K3 = 8


def keep_indices(key, length, count):
    scores = jax.random.randint(key, (length,), 0, 1 << 20, dtype=jnp.int32) * length + jnp.arange(length, dtype=jnp.int32)
    position = jnp.arange(length, dtype=jnp.int32)
    ends = (position == 0) | (position == length - 1)
    scores = jnp.where(ends, jnp.int32(2 ** 30) + position, scores)
    order = jnp.argsort(-scores, stable=True)
    picked = order[:count].astype(jnp.int32)
    return jnp.sort(picked).astype(jnp.int32)


def draw_keep_first(key, part):
    key = jax.random.fold_in(key, 11)
    return keep_indices(key, A, K1)


def draw_keep_second(key, part):
    key = jax.random.fold_in(key, 23)
    return keep_indices(key, B, K2)


def draw_keep_third(key, part):
    key = jax.random.fold_in(key, 37)
    return keep_indices(key, C, K3)


def steps_of(rng, dims, shards, smallest, high):
    gain = 1.0
    for dim, shards_of in shards:
        heights = jax.random.uniform(jax.random.fold_in(jax.random.fold_in(rng, 6), dim), (shards_of,), jnp.float32, smallest / len(shards), high / len(shards))
        gain = gain * jnp.repeat(jnp.exp(heights), dims[dim] // shards_of).reshape((-1,) + (1,) * (len(dims) - 1 - dim))
    return gain


def gaussian(rng, extent, scale, most, shards=(), kind=jnp.bfloat16):
    gain = steps_of(rng, extent, shards, -0.22, 0.18) if shards else 1.0
    drawn = jax.random.normal(rng, extent, jnp.float32) * scale * gain
    return jnp.minimum(jnp.maximum(drawn, -most), most).astype(kind)


def setup_inputs(seed: int = 0, part: int = 0) -> dict:
    arg_keys = jax.random.split(jax.random.key(seed), 9)
    part_splits = jax.random.split(jax.random.fold_in(arg_keys[8], part), 9)
    projections = gaussian(part_splits[0], (3, D, TOKENS), 1.0, 6.0, ((1, 2), (2, 16)))
    short_taps = gaussian(arg_keys[1], (3, 3, D), 0.6, 4.0, ((2, 2),), jnp.float32)
    skip_gain = gaussian(arg_keys[2], (D,), 1.0, 5.0, ((0, 2),), jnp.float32)
    filter_spec = gaussian(arg_keys[3], (2, D, K3, K2 * K1), 3.0, 18.0, ((1, 32),))
    keep_first = draw_keep_first(jax.random.fold_in(arg_keys[8], 71), part)
    keep_second = draw_keep_second(jax.random.fold_in(arg_keys[8], 71), part)
    keep_third = draw_keep_third(jax.random.fold_in(arg_keys[8], 71), part)
    out_weight = gaussian(arg_keys[7], (D, D), D ** -0.5, 0.375, ((1, 2),))
    return {"projections": projections, "short_taps": short_taps, "skip_gain": skip_gain, "filter_spec": filter_spec, "keep_first": keep_first, "keep_second": keep_second, "keep_third": keep_third, "out_weight": out_weight}


def product(form, left, right):
    return jnp.einsum(form, left.astype(jnp.float32), right.astype(jnp.float32))

def complex_product(form, left, right):
    real = product(form, left[0], right[0]) - product(form, left[1], right[1])
    imag = product(form, left[0], right[1]) + product(form, left[1], right[0])
    return (real, imag)

def rotate(value, turn):
    real = value[0] * turn[0] - value[1] * turn[1]
    imag = value[0] * turn[1] + value[1] * turn[0]
    return (real.astype(jnp.bfloat16), imag.astype(jnp.bfloat16))

def fourier_table(row_index, col_index, length, direction):
    angles = (row_index[:, None] * col_index[None, :] % length).astype(jnp.float32) * (2.0 * math.pi / length)
    factor = 1.0 / math.sqrt(length)
    return ((jnp.cos(angles) * factor).astype(jnp.bfloat16), (direction * jnp.sin(angles) * factor).astype(jnp.bfloat16))

def twiddle(counts, length, direction):
    angles = (counts % length).astype(jnp.float32) * (2.0 * math.pi / length)
    return (jnp.cos(angles), direction * jnp.sin(angles))

def spectral_tables(keep_first, keep_second, keep_third, size_a, size_b, size_c):
    full_length = size_a * size_b * size_c
    half_index = jnp.arange(size_a // 2, dtype=jnp.int32)
    index_b = jnp.arange(size_b, dtype=jnp.int32)
    index_c = jnp.arange(size_c, dtype=jnp.int32)
    table_first = fourier_table(keep_first, half_index, size_a, -1.0)
    table_second = fourier_table(keep_second, index_b, size_b, -1.0)
    table_third = fourier_table(keep_third, index_c, size_c, -1.0)
    inverse_first = fourier_table(half_index, keep_first, size_a, 1.0)
    inverse_second = fourier_table(index_b, keep_second, size_b, 1.0)
    inverse_third = fourier_table(index_c, keep_third, size_c, 1.0)
    counts_one = keep_first[:, None] * index_b[None, :]
    turn_one = twiddle(counts_one[:, :, None], size_a * size_b, -1.0)
    undo_one = twiddle(counts_one.T[:, None, :], size_a * size_b, 1.0)
    frequency = keep_first[None, :] + size_a * keep_second[:, None]
    counts_two = frequency[:, :, None] * index_c[None, None, :]
    turn_two = twiddle(counts_two, full_length, -1.0)
    undo_two = twiddle(jnp.transpose(counts_two, (2, 0, 1)), full_length, 1.0)
    return (table_first, table_second, table_third, inverse_first, inverse_second, inverse_third, turn_one, undo_one, turn_two, undo_two)

def long_conv(signal_row, spectrum_real, spectrum_imag, tables, size_a, size_b, size_c):
    table_first, table_second, table_third, inverse_first, inverse_second, inverse_third, turn_one, undo_one, turn_two, undo_two = tables
    signal = signal_row.reshape(size_a // 2, size_b * size_c)
    count_first = table_first[0].shape[0]
    first_real = product('kn,nm->km', table_first[0], signal).reshape(count_first, size_b, size_c)
    first_imag = product('kn,nm->km', table_first[1], signal).reshape(count_first, size_b, size_c)
    section_one = rotate((first_real, first_imag), turn_one)
    section_two = rotate(complex_product('qn,pnc->qpc', table_second, section_one), turn_two)
    summed = complex_product('rc,qpc->rqp', table_third, section_two)
    spectrum = rotate(summed, (spectrum_real.astype(jnp.float32), spectrum_imag.astype(jnp.float32)))
    back_one = rotate(complex_product('cr,rqp->cqp', inverse_third, spectrum), undo_two)
    back_two = rotate(complex_product('nq,cqp->ncp', inverse_second, back_one), undo_one)
    signal_out = product('mp,ncp->mnc', inverse_first[0], back_two[0]) - product('mp,ncp->mnc', inverse_first[1], back_two[1])
    return signal_out.reshape(-1).astype(jnp.bfloat16)

def short_filter(projections, short_taps):
    values = projections.astype(jnp.float32)
    zeros = jnp.zeros((values.shape[0], values.shape[1], 2), jnp.float32)
    extended = jnp.concatenate([zeros, values], axis=2)
    return short_taps[:, 0, :, None] * extended[:, :, 2:] + short_taps[:, 1, :, None] * extended[:, :, 1:-1] + short_taps[:, 2, :, None] * extended[:, :, :-2]

def reference(projections, short_taps, skip_gain, filter_spec, keep_first, keep_second, keep_third, out_weight):
    filtered = short_filter(projections, short_taps)
    gated_values = (filtered[1] * filtered[0]).astype(jnp.bfloat16)
    tables = spectral_tables(keep_first, keep_second, keep_third, A, B, C)

    def one_channel(members):
        spec_real = members[1].reshape(K3, K2, K1)
        spec_imag = members[2].reshape(K3, K2, K1)
        return long_conv(members[0], spec_real, spec_imag, tables, A, B, C)
    conv_rows = lax.map(one_channel, (gated_values, filter_spec[0], filter_spec[1]))
    long_part = conv_rows.astype(jnp.float32)
    gated_mix = (filtered[2] * (long_part + skip_gain[:, None] * gated_values.astype(jnp.float32))).astype(jnp.bfloat16)
    return jnp.dot(out_weight.T, gated_mix, preferred_element_type=jnp.float32).astype(jnp.bfloat16)
```

```python
import functools
import math

import jax
import jax.numpy as jnp
from jax import lax
from jax.experimental import pallas as pl
from jax.experimental.pallas import tpu as pltpu
from jax.sharding import PartitionSpec as P

A = 128
B = 128
LANES = 128
SLAB = 16
PARTS = 2


def passed_along(value, axis, steps):
    count = lax.axis_size(axis)
    leading, last = (max(0, -steps), min(count, count - steps))
    return lax.ppermute(value, axis, [(source, source + steps) for source in range(leading, last)])


def fourier_table(row_index, col_index, length, direction):
    angles = (row_index[:, None] * col_index[None, :] % length).astype(jnp.float32) * (
        2.0 * math.pi / length
    )
    factor = 1.0 / math.sqrt(length)
    return (
        (jnp.cos(angles) * factor).astype(jnp.bfloat16),
        (direction * jnp.sin(angles) * factor).astype(jnp.bfloat16),
    )


def twiddle(counts, length, direction):
    angles = (counts % length).astype(jnp.float32) * (2.0 * math.pi / length)
    return (jnp.cos(angles), direction * jnp.sin(angles))


def pad_to(value, axis, size):
    widths = [(0, 0)] * value.ndim
    widths[axis] = (0, size - value.shape[axis])
    return jnp.pad(value, widths)


def slab_kron(table):
    rows, cols = table.shape
    eye = jnp.eye(SLAB, dtype=table.dtype)
    return (table[:, None, :, None] * eye[None, :, None, :]).reshape(rows * SLAB, cols * SLAB)


def conv_tables(keep_first, keep_second, keep_third, size_c, sources, per_source):
    full_length = A * B * size_c
    half = jnp.arange(A // 2, dtype=jnp.int32).reshape(sources, per_source).T.reshape(-1)
    index_b = jnp.arange(B, dtype=jnp.int32)
    index_c = jnp.arange(size_c, dtype=jnp.int32)
    count_one = keep_first.shape[0]
    first = jnp.concatenate(fourier_table(keep_first, half, A, -1.0), axis=0)
    sr, si = (pad_to(part.T, 1, LANES) for part in fourier_table(keep_second, index_b, B, -1.0))
    second = jnp.concatenate(
        [jnp.concatenate([sr, si], axis=1), jnp.concatenate([-si, sr], axis=1)], axis=0
    )
    tr, ti = fourier_table(keep_third, index_c, size_c, -1.0)
    third = jnp.concatenate([slab_kron(tr), slab_kron(ti)], axis=0)
    vr, vi = (slab_kron(part) for part in fourier_table(index_c, keep_third, size_c, 1.0))
    undo_third = jnp.concatenate(
        [jnp.concatenate([vr, -vi], axis=1), jnp.concatenate([vi, vr], axis=1)], axis=0
    )
    ur, ui = (pad_to(part.T, 0, LANES) for part in fourier_table(index_b, keep_second, B, 1.0))
    undo_second = jnp.concatenate(
        [jnp.concatenate([ur, ui], axis=1), jnp.concatenate([-ui, ur], axis=1)], axis=0
    )
    fr, fi = fourier_table(half, keep_first, A, 1.0)
    undo_first = jnp.concatenate([fr, -fi], axis=1)
    turn_one = twiddle(keep_first[:, None] * index_b[None, :], A * B, -1.0)
    k2 = pad_to(keep_second, 0, LANES)
    k1 = keep_first.reshape(count_one // SLAB, 1, SLAB, 1)
    counts_two = (k1 + A * k2) * index_c[None, :, None, None]
    turn_two = twiddle(
        counts_two.reshape(count_one // SLAB, size_c * SLAB, LANES), full_length, -1.0
    )
    return (first, *turn_one, second, *turn_two, third, undo_third, undo_second, undo_first)


def dot(left, right):
    return jnp.dot(left, right, preferred_element_type=jnp.float32)


def conv_kernel(
    size_c,
    x_ref,
    filt_ref,
    first,
    one_re,
    one_im,
    second,
    two_re,
    two_im,
    third,
    undo_third,
    undo_second,
    undo_first,
    out_ref,
    held,
    back,
):
    width = B * size_c
    sources = x_ref.shape[1]
    per_source = x_ref.shape[2] // width
    count_one = one_re.shape[0]
    slabs = count_one // SLAB
    rows = size_c * SLAB
    kept = filt_ref.shape[3]
    x = jnp.concatenate(
        [x_ref[0, :, j * width : (j + 1) * width] for j in range(per_source)], axis=0
    )
    section = dot(first[...], x)
    for n3 in range(size_c):
        lanes = slice(n3 * LANES, (n3 + 1) * LANES)
        re, im = section[:count_one, lanes], section[count_one:, lanes]
        turned_re = (re * one_re[...] - im * one_im[...]).astype(jnp.bfloat16)
        turned_im = (re * one_im[...] + im * one_re[...]).astype(jnp.bfloat16)
        for s in range(slabs):
            at = slice(n3 * SLAB, (n3 + 1) * SLAB)
            held[s, at, :LANES] = turned_re[s * SLAB : (s + 1) * SLAB]
            held[s, at, LANES:] = turned_im[s * SLAB : (s + 1) * SLAB]
    for s in range(slabs):
        value = dot(held[s], second[...])
        re, im = value[:, :LANES], value[:, LANES:]
        tr, ti = two_re[s], two_im[s]
        value = jnp.concatenate([re * tr - im * ti, re * ti + im * tr], axis=1).astype(jnp.bfloat16)
        value = dot(third[...], value)
        re = value[:kept, :LANES] - value[kept:, LANES:]
        im = value[:kept, LANES:] + value[kept:, :LANES]
        hr = filt_ref[0, 0, s].astype(jnp.float32)
        hi = filt_ref[1, 0, s].astype(jnp.float32)
        value = jnp.concatenate([re * hr - im * hi, re * hi + im * hr], axis=0).astype(jnp.bfloat16)
        value = dot(undo_third[...], value)
        re, im = value[:rows], value[rows:]
        value = jnp.concatenate([re * tr + im * ti, im * tr - re * ti], axis=1).astype(jnp.bfloat16)
        value = dot(value, undo_second[...])
        here = slice(s * SLAB, (s + 1) * SLAB)
        there = slice(count_one + s * SLAB, count_one + (s + 1) * SLAB)
        ur, ui = one_re[here], one_im[here]
        for n3 in range(size_c):
            lanes = slice(n3 * LANES, (n3 + 1) * LANES)
            re = value[n3 * SLAB : (n3 + 1) * SLAB, :LANES]
            im = value[n3 * SLAB : (n3 + 1) * SLAB, LANES:]
            back[here, lanes] = (re * ur + im * ui).astype(jnp.bfloat16)
            back[there, lanes] = (im * ur - re * ui).astype(jnp.bfloat16)
    result = dot(undo_first[...], back[...]).astype(jnp.bfloat16)
    for j in range(per_source):
        out_ref[0, :, j * width : (j + 1) * width] = result[j * sources : (j + 1) * sources]


def whole_block(array):
    zeros = (0,) * array.ndim
    return pl.BlockSpec(array.shape, lambda d: zeros)


def convolve(rows, filt, tables, size_c):
    channels, sources, tokens = rows.shape
    _, _, slabs, kept, _ = filt.shape
    count_one = slabs * SLAB
    return pl.pallas_call(
        functools.partial(conv_kernel, size_c),
        out_shape=jax.ShapeDtypeStruct(rows.shape, jnp.bfloat16),
        grid=(channels,),
        in_specs=[
            pl.BlockSpec((1, sources, tokens), lambda d: (d, 0, 0)),
            pl.BlockSpec((2, 1, slabs, kept, LANES), lambda d: (0, d, 0, 0, 0)),
        ]
        + [whole_block(table) for table in tables],
        out_specs=pl.BlockSpec((1, sources, tokens), lambda d: (d, 0, 0)),
        scratch_shapes=[
            pltpu.VMEM((slabs, size_c * SLAB, 2 * LANES), jnp.bfloat16),
            pltpu.VMEM((2 * count_one, B * size_c), jnp.bfloat16),
        ],
        compiler_params=pltpu.CompilerParams(vmem_limit_bytes=56 * 2**20),
        cost_estimate=pl.CostEstimate(
            flops=channels * 400_000_000, bytes_accessed=8 * 2**20, transcendentals=0
        ),
        name="spectral_conv",
    )(rows, filt, *tables)


def order_matrix(size_c):
    width = B * size_c
    row = lax.broadcasted_iota(jnp.int32, (width, width), 0)
    col = lax.broadcasted_iota(jnp.int32, (width, width), 1)
    return (col == row % size_c * B + row // size_c).astype(jnp.bfloat16)


def reordered(value, order, size_c, back):
    width = B * size_c
    if order is None:
        split = (size_c, B) if back else (B, size_c)
        shaped = value.reshape(value.shape[0], -1, *split)
        return jnp.swapaxes(shaped, 2, 3).reshape(value.shape)
    form = "dw,vw->dv" if back else "dv,vw->dw"
    pieces = [
        jnp.einsum(
            form, value[:, at : at + width], order, preferred_element_type=jnp.float32
        ).astype(jnp.bfloat16)
        for at in range(0, value.shape[1], width)
    ]
    return jnp.concatenate(pieces, axis=1)


def on_device(
    projections, short_taps, skip_gain, filter_spec, keep_first, keep_second, keep_third, out_weight
):
    tokens_here = projections.shape[2]
    ring = ("seq", "sub")
    sources = lax.axis_size(ring)
    channels = projections.shape[1] // sources
    size_c = 2 * tokens_here * sources // (A * B)
    width = B * size_c
    per_source = tokens_here // width
    count_one, count_two, count_three = (
        keep_first.shape[0],
        keep_second.shape[0],
        keep_third.shape[0],
    )
    order = order_matrix(size_c) if width <= 4096 else None

    before = passed_along(projections[:, :, tokens_here - 2 :], ring, 1)
    extended = jnp.concatenate([before, projections], axis=2).astype(jnp.float32)
    filtered = (
        short_taps[:, 0, :, None] * extended[:, :, 2:]
        + short_taps[:, 1, :, None] * extended[:, :, 1:-1]
        + short_taps[:, 2, :, None] * extended[:, :, :-2]
    )
    gated_values = (filtered[1] * filtered[0]).astype(jnp.bfloat16)

    outgoing = reordered(gated_values, order, size_c, False)
    received = lax.all_to_all(
        outgoing.reshape(sources, channels, tokens_here), ring, split_axis=0, concat_axis=0
    )
    rows = jnp.swapaxes(received, 0, 1)

    filt = filter_spec.reshape(2, channels, count_three, count_two, count_one // SLAB, SLAB)
    filt = pad_to(jnp.transpose(filt, (0, 1, 4, 2, 5, 3)), 5, LANES)
    filt = filt.reshape(2, channels, count_one // SLAB, count_three * SLAB, LANES)
    tables = conv_tables(keep_first, keep_second, keep_third, size_c, sources, per_source)
    conv_rows = convolve(rows, filt, tables, size_c)

    conv_out = jnp.swapaxes(conv_rows, 0, 1)
    parts = PARTS if per_source % PARTS == 0 else 1
    step = tokens_here // parts
    mixed = []
    for part in range(parts):
        span = slice(part * step, (part + 1) * step)
        returned = lax.all_to_all(conv_out[:, :, span], ring, split_axis=0, concat_axis=0)
        token_major = reordered(returned.reshape(sources * channels, step), order, size_c, True)
        gated_mix = (
            filtered[2][:, span]
            * (
                token_major.astype(jnp.float32)
                + skip_gain[:, None] * gated_values[:, span].astype(jnp.float32)
            )
        ).astype(jnp.bfloat16)
        gathered = lax.all_gather(gated_mix, "chan", axis=0, tiled=True)
        mixed.append(
            jnp.einsum(
                "de,dt->et", out_weight, gathered, preferred_element_type=jnp.float32
            ).astype(jnp.bfloat16)
        )
    return jnp.concatenate(mixed, axis=1)


def solution(mesh):
    placed = (
        P(None, "chan", ("groups", "seq", "sub")),
        P(None, None, "chan"),
        P("chan"),
        P(None, ("chan", "seq", "sub"), None, None),
        P(),
        P(),
        P(),
        P(None, "chan"),
    )
    return jax.shard_map(
        on_device,
        mesh=mesh,
        in_specs=placed,
        out_specs=P("chan", ("groups", "seq", "sub")),
        check_vma=False,
    )
```

```python
import functools
import math

import jax
import jax.numpy as jnp
from jax import lax
from jax.experimental import pallas as pl
from jax.experimental.pallas import tpu as pltpu
from jax.sharding import PartitionSpec as P

A = 128
B = 128
LANES = 128
SLAB = 16
PARTS = 2


def passed_along(value, axis, steps):
    count = lax.axis_size(axis)
    leading, last = (max(0, -steps), min(count, count - steps))
    return lax.ppermute(value, axis, [(source, source + steps) for source in range(leading, last)])


def fourier_table(row_index, col_index, length, direction):
    angles = (row_index[:, None] * col_index[None, :] % length).astype(jnp.float32) * (
        2.0 * math.pi / length
    )
    factor = 1.0 / math.sqrt(length)
    return (
        (jnp.cos(angles) * factor).astype(jnp.bfloat16),
        (direction * jnp.sin(angles) * factor).astype(jnp.bfloat16),
    )


def twiddle(counts, length, direction):
    angles = (counts % length).astype(jnp.float32) * (2.0 * math.pi / length)
    return (jnp.cos(angles), direction * jnp.sin(angles))


def pad_to(value, axis, size):
    widths = [(0, 0)] * value.ndim
    widths[axis] = (0, size - value.shape[axis])
    return jnp.pad(value, widths)


def slab_kron(table):
    rows, cols = table.shape
    eye = jnp.eye(SLAB, dtype=table.dtype)
    return (table[:, None, :, None] * eye[None, :, None, :]).reshape(rows * SLAB, cols * SLAB)


def conv_tables(keep_first, keep_second, keep_third, size_c, sources, per_source):
    full_length = A * B * size_c
    half = jnp.arange(A // 2, dtype=jnp.int32).reshape(sources, per_source).T.reshape(-1)
    index_b = jnp.arange(B, dtype=jnp.int32)
    index_c = jnp.arange(size_c, dtype=jnp.int32)
    count_one = keep_first.shape[0]
    first = jnp.concatenate(fourier_table(keep_first, half, A, -1.0), axis=0)
    sr, si = (pad_to(part.T, 1, LANES) for part in fourier_table(keep_second, index_b, B, -1.0))
    second = jnp.concatenate(
        [jnp.concatenate([sr, si], axis=1), jnp.concatenate([-si, sr], axis=1)], axis=0
    )
    tr, ti = fourier_table(keep_third, index_c, size_c, -1.0)
    third = jnp.concatenate([slab_kron(tr), slab_kron(ti)], axis=0)
    vr, vi = (slab_kron(part) for part in fourier_table(index_c, keep_third, size_c, 1.0))
    undo_third = jnp.concatenate(
        [jnp.concatenate([vr, -vi], axis=1), jnp.concatenate([vi, vr], axis=1)], axis=0
    )
    ur, ui = (pad_to(part.T, 0, LANES) for part in fourier_table(index_b, keep_second, B, 1.0))
    undo_second = jnp.concatenate(
        [jnp.concatenate([ur, ui], axis=1), jnp.concatenate([-ui, ur], axis=1)], axis=0
    )
    fr, fi = fourier_table(half, keep_first, A, 1.0)
    undo_first = jnp.concatenate([fr, -fi], axis=1)
    turn_one = twiddle(keep_first[:, None] * index_b[None, :], A * B, -1.0)
    k2 = pad_to(keep_second, 0, LANES)
    k1 = keep_first.reshape(count_one // SLAB, 1, SLAB, 1)
    counts_two = (k1 + A * k2) * index_c[None, :, None, None]
    turn_two = twiddle(
        counts_two.reshape(count_one // SLAB, size_c * SLAB, LANES), full_length, -1.0
    )
    return (first, *turn_one, second, *turn_two, third, undo_third, undo_second, undo_first)


def dot(left, right):
    return jnp.dot(left, right, preferred_element_type=jnp.float32)


def conv_kernel(
    size_c,
    x_ref,
    filt_ref,
    first,
    one_re,
    one_im,
    second,
    two_re,
    two_im,
    third,
    undo_third,
    undo_second,
    undo_first,
    out_ref,
    held,
    back,
):
    width = B * size_c
    sources = x_ref.shape[1]
    per_source = x_ref.shape[2] // width
    count_one = one_re.shape[0]
    slabs = count_one // SLAB
    rows = size_c * SLAB
    kept = filt_ref.shape[3]
    x = jnp.concatenate(
        [x_ref[0, :, j * width : (j + 1) * width] for j in range(per_source)], axis=0
    )
    section = dot(first[...], x)
    for n3 in range(size_c):
        lanes = slice(n3 * LANES, (n3 + 1) * LANES)
        re, im = section[:count_one, lanes], section[count_one:, lanes]
        turned_re = (re * one_re[...] - im * one_im[...]).astype(jnp.bfloat16)
        turned_im = (re * one_im[...] + im * one_re[...]).astype(jnp.bfloat16)
        for s in range(slabs):
            at = slice(n3 * SLAB, (n3 + 1) * SLAB)
            held[s, at, :LANES] = turned_re[s * SLAB : (s + 1) * SLAB]
            held[s, at, LANES:] = turned_im[s * SLAB : (s + 1) * SLAB]
    for s in range(slabs):
        value = dot(held[s], second[...])
        re, im = value[:, :LANES], value[:, LANES:]
        tr, ti = two_re[s], two_im[s]
        value = jnp.concatenate([re * tr - im * ti, re * ti + im * tr], axis=1).astype(jnp.bfloat16)
        value = dot(third[...], value)
        re = value[:kept, :LANES] - value[kept:, LANES:]
        im = value[:kept, LANES:] + value[kept:, :LANES]
        hr = filt_ref[0, 0, s].astype(jnp.float32)
        hi = filt_ref[1, 0, s].astype(jnp.float32)
        value = jnp.concatenate([re * hr - im * hi, re * hi + im * hr], axis=0).astype(jnp.bfloat16)
        value = dot(undo_third[...], value)
        re, im = value[:rows], value[rows:]
        value = jnp.concatenate([re * tr + im * ti, im * tr - re * ti], axis=1).astype(jnp.bfloat16)
        value = dot(value, undo_second[...])
        here = slice(s * SLAB, (s + 1) * SLAB)
        there = slice(count_one + s * SLAB, count_one + (s + 1) * SLAB)
        ur, ui = one_re[here], one_im[here]
        for n3 in range(size_c):
            lanes = slice(n3 * LANES, (n3 + 1) * LANES)
            re = value[n3 * SLAB : (n3 + 1) * SLAB, :LANES]
            im = value[n3 * SLAB : (n3 + 1) * SLAB, LANES:]
            back[here, lanes] = (re * ur + im * ui).astype(jnp.bfloat16)
            back[there, lanes] = (im * ur - re * ui).astype(jnp.bfloat16)
    result = dot(undo_first[...], back[...]).astype(jnp.bfloat16)
    for j in range(per_source):
        out_ref[0, :, j * width : (j + 1) * width] = result[j * sources : (j + 1) * sources]


def whole_block(array):
    zeros = (0,) * array.ndim
    return pl.BlockSpec(array.shape, lambda d: zeros)


def convolve(rows, filt, tables, size_c):
    channels, sources, tokens = rows.shape
    _, _, slabs, kept, _ = filt.shape
    count_one = slabs * SLAB
    return pl.pallas_call(
        functools.partial(conv_kernel, size_c),
        out_shape=jax.ShapeDtypeStruct(rows.shape, jnp.bfloat16),
        grid=(channels,),
        in_specs=[
            pl.BlockSpec((1, sources, tokens), lambda d: (d, 0, 0)),
            pl.BlockSpec((2, 1, slabs, kept, LANES), lambda d: (0, d, 0, 0, 0)),
        ]
        + [whole_block(table) for table in tables],
        out_specs=pl.BlockSpec((1, sources, tokens), lambda d: (d, 0, 0)),
        scratch_shapes=[
            pltpu.VMEM((slabs, size_c * SLAB, 2 * LANES), jnp.bfloat16),
            pltpu.VMEM((2 * count_one, B * size_c), jnp.bfloat16),
        ],
        compiler_params=pltpu.CompilerParams(vmem_limit_bytes=56 * 2**20),
        cost_estimate=pl.CostEstimate(
            flops=channels * 400_000_000, bytes_accessed=8 * 2**20, transcendentals=0
        ),
        name="spectral_conv",
    )(rows, filt, *tables)


def order_matrix(size_c):
    width = B * size_c
    col = jnp.arange(width, dtype=jnp.int32)
    origin = jnp.swapaxes(col.reshape(B, size_c), 0, 1).reshape(-1)
    return (col[:, None] == origin[None, :]).astype(jnp.bfloat16)


def short_filter(taps, which, before, block):
    extended = jnp.concatenate([before, block], axis=1).astype(jnp.float32)
    at = 3 * which
    total = taps[:, at : at + 1] * extended[:, LANES:]
    total += taps[:, at + 1 : at + 2] * pltpu.roll(extended, 1, 1)[:, LANES:]
    return total + taps[:, at + 2 : at + 3] * pltpu.roll(extended, 2, 1)[:, LANES:]


def head_kernel(halo, taps, order, ahead, block, gated_ref, sent_ref):
    first = pl.program_id(0) == 0
    filtered = [
        short_filter(taps, p, jnp.where(first, halo[p], ahead[p]), block[p]) for p in range(2)
    ]
    gated = (filtered[1] * filtered[0]).astype(jnp.bfloat16)
    gated_ref[...] = gated
    sent_ref[...] = dot(gated, order[...]).astype(jnp.bfloat16)


def head(projections, halo, taps, order):
    _, channels, tokens = projections.shape
    width = order.shape[0]
    per_block = width // LANES
    block = pl.BlockSpec((channels, width), lambda j: (0, j))
    shape = jax.ShapeDtypeStruct((channels, tokens), jnp.bfloat16)
    return pl.pallas_call(
        head_kernel,
        out_shape=(shape, shape),
        grid=(tokens // width,),
        in_specs=[
            whole_block(halo),
            whole_block(taps),
            whole_block(order),
            pl.BlockSpec(
                (2, channels, LANES), lambda j: (0, 0, jnp.maximum(j * per_block - 1, 0))
            ),
            pl.BlockSpec((2, channels, width), lambda j: (0, 0, j)),
        ],
        out_specs=(block, block),
        compiler_params=pltpu.CompilerParams(vmem_limit_bytes=56 * 2**20),
        cost_estimate=pl.CostEstimate(
            flops=2 * channels * tokens * width, bytes_accessed=16 * 2**20, transcendentals=0
        ),
        name="gate_and_reorder",
    )(halo, taps, order, projections, projections)


def tail_kernel(base, halo, taps, skip, order, ahead, block, gated, returned, out_ref):
    first = pl.program_id(0) + base == 0
    filtered = short_filter(taps, 2, jnp.where(first, halo[2], ahead[0]), block[0])
    conv = lax.dot_general(
        returned[...], order[...], (((1,), (1,)), ((), ())), preferred_element_type=jnp.float32
    )
    mix = filtered * (conv + skip[...] * gated[...].astype(jnp.float32))
    out_ref[...] = mix.astype(jnp.bfloat16)


def tail(projections, halo, taps, skip, order, gated, returned, base):
    channels, tokens = returned.shape
    width = order.shape[0]
    per_block = width // LANES
    return pl.pallas_call(
        functools.partial(tail_kernel, base),
        out_shape=jax.ShapeDtypeStruct((channels, tokens), jnp.bfloat16),
        grid=(tokens // width,),
        in_specs=[
            whole_block(halo),
            whole_block(taps),
            whole_block(skip),
            whole_block(order),
            pl.BlockSpec(
                (1, channels, LANES),
                lambda j: (2, 0, jnp.maximum((j + base) * per_block - 1, 0)),
            ),
            pl.BlockSpec((1, channels, width), lambda j: (2, 0, j + base)),
            pl.BlockSpec((channels, width), lambda j: (0, j + base)),
            pl.BlockSpec((channels, width), lambda j: (0, j)),
        ],
        out_specs=pl.BlockSpec((channels, width), lambda j: (0, j)),
        compiler_params=pltpu.CompilerParams(vmem_limit_bytes=56 * 2**20),
        cost_estimate=pl.CostEstimate(
            flops=2 * channels * tokens * width, bytes_accessed=12 * 2**20, transcendentals=0
        ),
        name="reorder_and_mix",
    )(halo, taps, skip, order, projections, projections, gated, returned)


def project(out_weight, gated_mix):
    count = lax.axis_size("chan")
    me = lax.axis_index("chan")
    depth = gated_mix.shape[0]
    held = [gated_mix] + [
        lax.ppermute(gated_mix, "chan", [(i, (i + k) % count) for i in range(count)])
        for k in range(1, count)
    ]
    total = 0.0
    for k, value in enumerate(held):
        owner = (me - k + count) % count
        weight = lax.dynamic_slice_in_dim(out_weight, owner * depth, depth, 0)
        total += jnp.einsum("de,dt->et", weight, value, preferred_element_type=jnp.float32)
    return total.astype(jnp.bfloat16)


def reordered(value, size_c, back):
    split = (size_c, B) if back else (B, size_c)
    shaped = value.reshape(value.shape[0], -1, *split)
    return jnp.swapaxes(shaped, 2, 3).reshape(value.shape)


def on_device(
    projections, short_taps, skip_gain, filter_spec, keep_first, keep_second, keep_third, out_weight
):
    tokens_here = projections.shape[2]
    ring = ("seq", "sub")
    sources = lax.axis_size(ring)
    channels = projections.shape[1] // sources
    size_c = 2 * tokens_here * sources // (A * B)
    width = B * size_c
    per_source = tokens_here // width
    count_one, count_two, count_three = (
        keep_first.shape[0],
        keep_second.shape[0],
        keep_third.shape[0],
    )
    order = order_matrix(size_c) if width <= 4096 else None

    before = passed_along(projections[:, :, tokens_here - 2 :], ring, 1)
    if order is None:
        extended = jnp.concatenate([before, projections], axis=2).astype(jnp.float32)
        filtered = (
            short_taps[:, 0, :, None] * extended[:, :, 2:]
            + short_taps[:, 1, :, None] * extended[:, :, 1:-1]
            + short_taps[:, 2, :, None] * extended[:, :, :-2]
        )
        gated_values = (filtered[1] * filtered[0]).astype(jnp.bfloat16)
        outgoing = reordered(gated_values, size_c, False)
    else:
        halo = jnp.pad(before, ((0, 0), (0, 0), (LANES - 2, 0)))
        taps = short_taps.reshape(9, -1).T
        gated_values, outgoing = head(projections, halo, taps, order)
    received = lax.all_to_all(
        outgoing.reshape(sources, channels, tokens_here), ring, split_axis=0, concat_axis=0
    )
    rows = jnp.swapaxes(received, 0, 1)

    filt = filter_spec.reshape(2, channels, count_three, count_two, count_one // SLAB, SLAB)
    filt = pad_to(jnp.transpose(filt, (0, 1, 4, 2, 5, 3)), 5, LANES)
    filt = filt.reshape(2, channels, count_one // SLAB, count_three * SLAB, LANES)
    tables = conv_tables(keep_first, keep_second, keep_third, size_c, sources, per_source)
    conv_rows = convolve(rows, filt, tables, size_c)

    conv_out = jnp.swapaxes(conv_rows, 0, 1)
    parts = PARTS if per_source % PARTS == 0 else 1
    step = tokens_here // parts
    mixed = []
    for part in range(parts):
        span = slice(part * step, (part + 1) * step)
        returned = lax.all_to_all(conv_out[:, :, span], ring, split_axis=0, concat_axis=0)
        returned = returned.reshape(sources * channels, step)
        if order is None:
            token_major = reordered(returned, size_c, True)
            gated_mix = (
                filtered[2][:, span]
                * (
                    token_major.astype(jnp.float32)
                    + skip_gain[:, None] * gated_values[:, span].astype(jnp.float32)
                )
            ).astype(jnp.bfloat16)
        else:
            gated_mix = tail(
                projections,
                halo,
                taps,
                skip_gain[:, None],
                order,
                gated_values,
                returned,
                part * (step // width),
            )
        mixed.append(project(out_weight, gated_mix))
    return jnp.concatenate(mixed, axis=1)


def solution(mesh):
    placed = (
        P(None, "chan", ("groups", "seq", "sub")),
        P(None, None, "chan"),
        P("chan"),
        P(None, ("chan", "seq", "sub"), None, None),
        P(),
        P(),
        P(),
        P(None, "chan"),
    )
    return jax.shard_map(
        on_device,
        mesh=mesh,
        in_specs=placed,
        out_specs=P("chan", ("groups", "seq", "sub")),
        check_vma=False,
    )
```

```python
import functools
import math

import jax
import jax.numpy as jnp
from jax import lax
from jax.experimental import pallas as pl
from jax.experimental.pallas import tpu as pltpu
from jax.sharding import PartitionSpec as P

A = 128
B = 128
LANES = 128
SLAB = 16
PARTS = 4


def passed_along(value, axis, steps):
    count = lax.axis_size(axis)
    leading, last = (max(0, -steps), min(count, count - steps))
    return lax.ppermute(value, axis, [(source, source + steps) for source in range(leading, last)])


def fourier_table(row_index, col_index, length, direction):
    angles = (row_index[:, None] * col_index[None, :] % length).astype(jnp.float32) * (
        2.0 * math.pi / length
    )
    factor = 1.0 / math.sqrt(length)
    return (
        (jnp.cos(angles) * factor).astype(jnp.bfloat16),
        (direction * jnp.sin(angles) * factor).astype(jnp.bfloat16),
    )


def twiddle(counts, length, direction):
    angles = (counts % length).astype(jnp.float32) * (2.0 * math.pi / length)
    return (jnp.cos(angles), direction * jnp.sin(angles))


def pad_to(value, axis, size):
    widths = [(0, 0)] * value.ndim
    widths[axis] = (0, size - value.shape[axis])
    return jnp.pad(value, widths)


def slab_kron(table):
    rows, cols = table.shape
    eye = jnp.eye(SLAB, dtype=table.dtype)
    return (table[:, None, :, None] * eye[None, :, None, :]).reshape(rows * SLAB, cols * SLAB)


def conv_tables(keep_first, keep_second, keep_third, size_c, sources, per_source):
    full_length = A * B * size_c
    half = jnp.arange(A // 2, dtype=jnp.int32).reshape(sources, per_source).T.reshape(-1)
    index_b = jnp.arange(B, dtype=jnp.int32)
    index_c = jnp.arange(size_c, dtype=jnp.int32)
    count_one = keep_first.shape[0]
    first = jnp.concatenate(fourier_table(keep_first, half, A, -1.0), axis=0)
    sr, si = (pad_to(part.T, 1, LANES) for part in fourier_table(keep_second, index_b, B, -1.0))
    second = jnp.concatenate(
        [jnp.concatenate([sr, si], axis=1), jnp.concatenate([-si, sr], axis=1)], axis=0
    )
    tr, ti = fourier_table(keep_third, index_c, size_c, -1.0)
    third = jnp.concatenate([slab_kron(tr), slab_kron(ti)], axis=0)
    vr, vi = (slab_kron(part) for part in fourier_table(index_c, keep_third, size_c, 1.0))
    undo_third = jnp.concatenate(
        [jnp.concatenate([vr, -vi], axis=1), jnp.concatenate([vi, vr], axis=1)], axis=0
    )
    ur, ui = (pad_to(part.T, 0, LANES) for part in fourier_table(index_b, keep_second, B, 1.0))
    undo_second = jnp.concatenate(
        [jnp.concatenate([ur, ui], axis=1), jnp.concatenate([-ui, ur], axis=1)], axis=0
    )
    fr, fi = fourier_table(half, keep_first, A, 1.0)
    undo_first = jnp.concatenate([fr, -fi], axis=1)
    turn_one = twiddle(keep_first[:, None] * index_b[None, :], A * B, -1.0)
    k2 = pad_to(keep_second, 0, LANES)
    k1 = keep_first.reshape(count_one // SLAB, 1, SLAB, 1)
    counts_two = (k1 + A * k2) * index_c[None, :, None, None]
    turn_two = twiddle(
        counts_two.reshape(count_one // SLAB, size_c * SLAB, LANES), full_length, -1.0
    )
    return (first, *turn_one, second, *turn_two, third, undo_third, undo_second, undo_first)


def dot(left, right):
    return jnp.dot(left, right, preferred_element_type=jnp.float32)


def conv_kernel(
    size_c,
    x_ref,
    filt_ref,
    first,
    one_re,
    one_im,
    second,
    two_re,
    two_im,
    third,
    undo_third,
    undo_second,
    undo_first,
    out_ref,
    held,
    back,
):
    width = B * size_c
    sources = x_ref.shape[1]
    per_source = x_ref.shape[2] // width
    count_one = one_re.shape[0]
    slabs = count_one // SLAB
    rows = size_c * SLAB
    kept = filt_ref.shape[3]
    x = jnp.concatenate(
        [x_ref[0, :, j * width : (j + 1) * width] for j in range(per_source)], axis=0
    )
    section = dot(first[...], x)
    for n3 in range(size_c):
        lanes = slice(n3 * LANES, (n3 + 1) * LANES)
        re, im = section[:count_one, lanes], section[count_one:, lanes]
        turned_re = (re * one_re[...] - im * one_im[...]).astype(jnp.bfloat16)
        turned_im = (re * one_im[...] + im * one_re[...]).astype(jnp.bfloat16)
        for s in range(slabs):
            at = slice(n3 * SLAB, (n3 + 1) * SLAB)
            held[s, at, :LANES] = turned_re[s * SLAB : (s + 1) * SLAB]
            held[s, at, LANES:] = turned_im[s * SLAB : (s + 1) * SLAB]
    for s in range(slabs):
        value = dot(held[s], second[...])
        re, im = value[:, :LANES], value[:, LANES:]
        tr, ti = two_re[s], two_im[s]
        value = jnp.concatenate([re * tr - im * ti, re * ti + im * tr], axis=1).astype(jnp.bfloat16)
        value = dot(third[...], value)
        re = value[:kept, :LANES] - value[kept:, LANES:]
        im = value[:kept, LANES:] + value[kept:, :LANES]
        hr = filt_ref[0, 0, s].astype(jnp.float32)
        hi = filt_ref[1, 0, s].astype(jnp.float32)
        value = jnp.concatenate([re * hr - im * hi, re * hi + im * hr], axis=0).astype(jnp.bfloat16)
        value = dot(undo_third[...], value)
        re, im = value[:rows], value[rows:]
        value = jnp.concatenate([re * tr + im * ti, im * tr - re * ti], axis=1).astype(jnp.bfloat16)
        value = dot(value, undo_second[...])
        here = slice(s * SLAB, (s + 1) * SLAB)
        there = slice(count_one + s * SLAB, count_one + (s + 1) * SLAB)
        ur, ui = one_re[here], one_im[here]
        for n3 in range(size_c):
            lanes = slice(n3 * LANES, (n3 + 1) * LANES)
            re = value[n3 * SLAB : (n3 + 1) * SLAB, :LANES]
            im = value[n3 * SLAB : (n3 + 1) * SLAB, LANES:]
            back[here, lanes] = (re * ur + im * ui).astype(jnp.bfloat16)
            back[there, lanes] = (im * ur - re * ui).astype(jnp.bfloat16)
    result = dot(undo_first[...], back[...]).astype(jnp.bfloat16)
    for j in range(per_source):
        out_ref[0, :, j * width : (j + 1) * width] = result[j * sources : (j + 1) * sources]


def whole_block(array):
    zeros = (0,) * array.ndim
    return pl.BlockSpec(array.shape, lambda d: zeros)


def convolve(rows, filt, tables, size_c):
    channels, sources, tokens = rows.shape
    _, _, slabs, kept, _ = filt.shape
    count_one = slabs * SLAB
    return pl.pallas_call(
        functools.partial(conv_kernel, size_c),
        out_shape=jax.ShapeDtypeStruct(rows.shape, jnp.bfloat16),
        grid=(channels,),
        in_specs=[
            pl.BlockSpec((1, sources, tokens), lambda d: (d, 0, 0)),
            pl.BlockSpec((2, 1, slabs, kept, LANES), lambda d: (0, d, 0, 0, 0)),
        ]
        + [whole_block(table) for table in tables],
        out_specs=pl.BlockSpec((1, sources, tokens), lambda d: (d, 0, 0)),
        scratch_shapes=[
            pltpu.VMEM((slabs, size_c * SLAB, 2 * LANES), jnp.bfloat16),
            pltpu.VMEM((2 * count_one, B * size_c), jnp.bfloat16),
        ],
        compiler_params=pltpu.CompilerParams(vmem_limit_bytes=56 * 2**20),
        cost_estimate=pl.CostEstimate(
            flops=channels * 400_000_000, bytes_accessed=8 * 2**20, transcendentals=0
        ),
        name="spectral_conv",
    )(rows, filt, *tables)


def order_matrix(size_c):
    width = B * size_c
    col = jnp.arange(width, dtype=jnp.int32)
    origin = jnp.swapaxes(col.reshape(B, size_c), 0, 1).reshape(-1)
    return (col[:, None] == origin[None, :]).astype(jnp.bfloat16)


def short_filter(taps, which, before, block):
    extended = jnp.concatenate([before, block], axis=1).astype(jnp.float32)
    at = 3 * which
    total = taps[:, at : at + 1] * extended[:, LANES:]
    total += taps[:, at + 1 : at + 2] * pltpu.roll(extended, 1, 1)[:, LANES:]
    return total + taps[:, at + 2 : at + 3] * pltpu.roll(extended, 2, 1)[:, LANES:]


def head_kernel(halo, taps, order, block, gated_ref, sent_ref, held):
    step = pl.program_id(0)
    width, columns = order.shape
    channels = block.shape[1]
    pieces = block.shape[2] // width

    @pl.when(step == 0)
    def _():
        for j in range(pieces):
            at = j * width
            filtered = []
            for p in range(2):
                before = halo[p] if j == 0 else block[p, :, at - LANES : at]
                filtered.append(short_filter(taps, p, before, block[p, :, at : at + width]))
            gated = (filtered[1] * filtered[0]).astype(jnp.bfloat16)
            gated_ref[:, at : at + width] = gated
            held[j * channels : (j + 1) * channels] = gated

    moved = dot(held[...], order[...]).astype(jnp.bfloat16)
    for j in range(pieces):
        lanes = pl.ds(pl.multiple_of(j * width + step * columns, LANES), columns)
        sent_ref[:, lanes] = moved[j * channels : (j + 1) * channels]


def head(projections, halo, taps, order):
    _, channels, tokens = projections.shape
    width = order.shape[0]
    columns = width // 4
    block = pl.BlockSpec((channels, tokens), lambda c: (0, 0))
    shape = jax.ShapeDtypeStruct((channels, tokens), jnp.bfloat16)
    return pl.pallas_call(
        head_kernel,
        out_shape=(shape, shape),
        grid=(width // columns,),
        in_specs=[
            whole_block(halo),
            whole_block(taps),
            pl.BlockSpec((width, columns), lambda c: (0, c)),
            pl.BlockSpec((2, channels, tokens), lambda c: (0, 0, 0)),
        ],
        out_specs=(block, block),
        scratch_shapes=[pltpu.VMEM((tokens // width * channels, width), jnp.bfloat16)],
        compiler_params=pltpu.CompilerParams(vmem_limit_bytes=56 * 2**20),
        cost_estimate=pl.CostEstimate(
            flops=2 * channels * tokens * width, bytes_accessed=16 * 2**20, transcendentals=0
        ),
        name="gate_and_reorder",
    )(halo, taps, order, projections)


def tail_kernel(base, halo, taps, skip, order, ahead, block, gated, returned, out_ref):
    first = pl.program_id(0) + base == 0
    filtered = short_filter(taps, 2, jnp.where(first, halo[2], ahead[0]), block[0])
    conv = lax.dot_general(
        returned[...], order[...], (((1,), (1,)), ((), ())), preferred_element_type=jnp.float32
    )
    mix = filtered * (conv + skip[...] * gated[...].astype(jnp.float32))
    out_ref[...] = mix.astype(jnp.bfloat16)


def tail(projections, halo, taps, skip, order, gated, returned, base):
    channels, tokens = returned.shape
    width = order.shape[0]
    per_block = width // LANES
    return pl.pallas_call(
        functools.partial(tail_kernel, base),
        out_shape=jax.ShapeDtypeStruct((channels, tokens), jnp.bfloat16),
        grid=(tokens // width,),
        in_specs=[
            whole_block(halo),
            whole_block(taps),
            whole_block(skip),
            whole_block(order),
            pl.BlockSpec(
                (1, channels, LANES),
                lambda j: (2, 0, jnp.maximum((j + base) * per_block - 1, 0)),
            ),
            pl.BlockSpec((1, channels, width), lambda j: (2, 0, j + base)),
            pl.BlockSpec((channels, width), lambda j: (0, j + base)),
            pl.BlockSpec((channels, width), lambda j: (0, j)),
        ],
        out_specs=pl.BlockSpec((channels, width), lambda j: (0, j)),
        compiler_params=pltpu.CompilerParams(vmem_limit_bytes=56 * 2**20),
        cost_estimate=pl.CostEstimate(
            flops=2 * channels * tokens * width, bytes_accessed=12 * 2**20, transcendentals=0
        ),
        name="reorder_and_mix",
    )(halo, taps, skip, order, projections, projections, gated, returned)


def project(out_weight, gated_mix):
    count = lax.axis_size("chan")
    me = lax.axis_index("chan")
    depth = gated_mix.shape[0]
    held = [gated_mix] + [
        lax.ppermute(gated_mix, "chan", [(i, (i + k) % count) for i in range(count)])
        for k in range(1, count)
    ]
    total = 0.0
    for k, value in enumerate(held):
        owner = (me - k + count) % count
        weight = lax.dynamic_slice_in_dim(out_weight, owner * depth, depth, 0)
        total += jnp.einsum("de,dt->et", weight, value, preferred_element_type=jnp.float32)
    return total.astype(jnp.bfloat16)


def reordered(value, size_c, back):
    split = (size_c, B) if back else (B, size_c)
    shaped = value.reshape(value.shape[0], -1, *split)
    return jnp.swapaxes(shaped, 2, 3).reshape(value.shape)


def on_device(
    projections, short_taps, skip_gain, filter_spec, keep_first, keep_second, keep_third, out_weight
):
    tokens_here = projections.shape[2]
    ring = ("seq", "sub")
    sources = lax.axis_size(ring)
    channels = projections.shape[1] // sources
    size_c = 2 * tokens_here * sources // (A * B)
    width = B * size_c
    per_source = tokens_here // width
    count_one, count_two, count_three = (
        keep_first.shape[0],
        keep_second.shape[0],
        keep_third.shape[0],
    )
    order = order_matrix(size_c) if width <= 4096 else None

    before = passed_along(projections[:, :, tokens_here - 2 :], ring, 1)
    if order is None:
        extended = jnp.concatenate([before, projections], axis=2).astype(jnp.float32)
        filtered = (
            short_taps[:, 0, :, None] * extended[:, :, 2:]
            + short_taps[:, 1, :, None] * extended[:, :, 1:-1]
            + short_taps[:, 2, :, None] * extended[:, :, :-2]
        )
        gated_values = (filtered[1] * filtered[0]).astype(jnp.bfloat16)
        outgoing = reordered(gated_values, size_c, False)
    else:
        halo = jnp.pad(before, ((0, 0), (0, 0), (LANES - 2, 0)))
        taps = short_taps.reshape(9, -1).T
        gated_values, outgoing = head(projections, halo, taps, order)
    received = lax.all_to_all(
        outgoing.reshape(sources, channels, tokens_here), ring, split_axis=0, concat_axis=0
    )
    rows = jnp.swapaxes(received, 0, 1)

    filt = filter_spec.reshape(2, channels, count_three, count_two, count_one // SLAB, SLAB)
    filt = pad_to(jnp.transpose(filt, (0, 1, 4, 2, 5, 3)), 5, LANES)
    filt = filt.reshape(2, channels, count_one // SLAB, count_three * SLAB, LANES)
    tables = conv_tables(keep_first, keep_second, keep_third, size_c, sources, per_source)
    conv_rows = convolve(rows, filt, tables, size_c)

    conv_out = jnp.swapaxes(conv_rows, 0, 1)
    parts = PARTS if per_source % PARTS == 0 else 1
    step = tokens_here // parts
    mixed = []
    ready = []
    for part in range(parts):
        span = slice(part * step, (part + 1) * step)
        leaving = conv_out[:, :, span]
        if part >= 2:
            leaving, _ = lax.optimization_barrier((leaving, ready[part - 2]))
        returned = lax.all_to_all(leaving, ring, split_axis=0, concat_axis=0)
        returned = returned.reshape(sources * channels, step)
        if order is None:
            token_major = reordered(returned, size_c, True)
            gated_mix = (
                filtered[2][:, span]
                * (
                    token_major.astype(jnp.float32)
                    + skip_gain[:, None] * gated_values[:, span].astype(jnp.float32)
                )
            ).astype(jnp.bfloat16)
        else:
            gated_mix = tail(
                projections,
                halo,
                taps,
                skip_gain[:, None],
                order,
                gated_values,
                returned,
                part * (step // width),
            )
        ready.append(gated_mix)
    mixed = [project(out_weight, gated_mix) for gated_mix in ready]
    return jnp.concatenate(mixed, axis=1)


def solution(mesh):
    placed = (
        P(None, "chan", ("groups", "seq", "sub")),
        P(None, None, "chan"),
        P("chan"),
        P(None, ("chan", "seq", "sub"), None, None),
        P(),
        P(),
        P(),
        P(None, "chan"),
    )
    return jax.shard_map(
        on_device,
        mesh=mesh,
        in_specs=placed,
        out_specs=P("chan", ("groups", "seq", "sub")),
        check_vma=False,
    )
```

```python
import functools
import math

import jax
import jax.numpy as jnp
from jax import lax
from jax.experimental import pallas as pl
from jax.experimental.pallas import tpu as pltpu
from jax.sharding import PartitionSpec as P

A = 128
B = 128
LANES = 128
SLAB = 16


def passed_along(value, axis, steps):
    count = lax.axis_size(axis)
    leading, last = (max(0, -steps), min(count, count - steps))
    return lax.ppermute(value, axis, [(source, source + steps) for source in range(leading, last)])


def fourier_table(row_index, col_index, length, direction):
    angles = (row_index[:, None] * col_index[None, :] % length).astype(jnp.float32) * (
        2.0 * math.pi / length
    )
    factor = 1.0 / math.sqrt(length)
    return (
        (jnp.cos(angles) * factor).astype(jnp.bfloat16),
        (direction * jnp.sin(angles) * factor).astype(jnp.bfloat16),
    )


def twiddle(counts, length, direction):
    angles = (counts % length).astype(jnp.float32) * (2.0 * math.pi / length)
    return (jnp.cos(angles), direction * jnp.sin(angles))


def pad_to(value, axis, size):
    widths = [(0, 0)] * value.ndim
    widths[axis] = (0, size - value.shape[axis])
    return jnp.pad(value, widths)


def slab_kron(table):
    rows, cols = table.shape
    eye = jnp.eye(SLAB, dtype=table.dtype)
    return (table[:, None, :, None] * eye[None, :, None, :]).reshape(rows * SLAB, cols * SLAB)


def conv_tables(keep_first, keep_second, keep_third, size_c, sources, per_source):
    full_length = A * B * size_c
    half = jnp.arange(A // 2, dtype=jnp.int32).reshape(sources, per_source).T.reshape(-1)
    index_b = jnp.arange(B, dtype=jnp.int32)
    index_c = jnp.arange(size_c, dtype=jnp.int32)
    count_one = keep_first.shape[0]
    first = jnp.concatenate(fourier_table(keep_first, half, A, -1.0), axis=0)
    sr, si = (pad_to(part.T, 1, LANES) for part in fourier_table(keep_second, index_b, B, -1.0))
    second = jnp.concatenate(
        [jnp.concatenate([sr, si], axis=1), jnp.concatenate([-si, sr], axis=1)], axis=0
    )
    tr, ti = fourier_table(keep_third, index_c, size_c, -1.0)
    third = jnp.concatenate([slab_kron(tr), slab_kron(ti)], axis=0)
    vr, vi = (slab_kron(part) for part in fourier_table(index_c, keep_third, size_c, 1.0))
    undo_third = jnp.concatenate(
        [jnp.concatenate([vr, -vi], axis=1), jnp.concatenate([vi, vr], axis=1)], axis=0
    )
    ur, ui = (pad_to(part.T, 0, LANES) for part in fourier_table(index_b, keep_second, B, 1.0))
    undo_second = jnp.concatenate(
        [jnp.concatenate([ur, ui], axis=1), jnp.concatenate([-ui, ur], axis=1)], axis=0
    )
    fr, fi = fourier_table(half, keep_first, A, 1.0)
    undo_first = jnp.concatenate([fr, -fi], axis=1)
    turn_one = twiddle(keep_first[:, None] * index_b[None, :], A * B, -1.0)
    k2 = pad_to(keep_second, 0, LANES)
    k1 = keep_first.reshape(count_one // SLAB, 1, SLAB, 1)
    counts_two = (k1 + A * k2) * index_c[None, :, None, None]
    turn_two = twiddle(
        counts_two.reshape(count_one // SLAB, size_c * SLAB, LANES), full_length, -1.0
    )
    return (first, *turn_one, second, *turn_two, third, undo_third, undo_second, undo_first)


def dot(left, right):
    return jnp.dot(left, right, preferred_element_type=jnp.float32)


def conv_kernel(
    size_c,
    x_ref,
    filt_ref,
    first,
    one_re,
    one_im,
    second,
    two_re,
    two_im,
    third,
    undo_third,
    undo_second,
    undo_first,
    out_ref,
    held,
    back,
):
    width = B * size_c
    sources = x_ref.shape[1]
    per_source = x_ref.shape[2] // width
    count_one = one_re.shape[0]
    slabs = count_one // SLAB
    rows = size_c * SLAB
    kept = filt_ref.shape[3]
    x = jnp.concatenate(
        [x_ref[0, :, j * width : (j + 1) * width] for j in range(per_source)], axis=0
    )
    section = dot(first[...], x)
    for n3 in range(size_c):
        lanes = slice(n3 * LANES, (n3 + 1) * LANES)
        re, im = section[:count_one, lanes], section[count_one:, lanes]
        turned_re = (re * one_re[...] - im * one_im[...]).astype(jnp.bfloat16)
        turned_im = (re * one_im[...] + im * one_re[...]).astype(jnp.bfloat16)
        for s in range(slabs):
            at = slice(n3 * SLAB, (n3 + 1) * SLAB)
            held[s, at, :LANES] = turned_re[s * SLAB : (s + 1) * SLAB]
            held[s, at, LANES:] = turned_im[s * SLAB : (s + 1) * SLAB]
    for s in range(slabs):
        value = dot(held[s], second[...])
        re, im = value[:, :LANES], value[:, LANES:]
        tr, ti = two_re[s], two_im[s]
        value = jnp.concatenate([re * tr - im * ti, re * ti + im * tr], axis=1).astype(jnp.bfloat16)
        value = dot(third[...], value)
        re = value[:kept, :LANES] - value[kept:, LANES:]
        im = value[:kept, LANES:] + value[kept:, :LANES]
        hr = filt_ref[0, 0, s].astype(jnp.float32)
        hi = filt_ref[1, 0, s].astype(jnp.float32)
        value = jnp.concatenate([re * hr - im * hi, re * hi + im * hr], axis=0).astype(jnp.bfloat16)
        value = dot(undo_third[...], value)
        re, im = value[:rows], value[rows:]
        value = jnp.concatenate([re * tr + im * ti, im * tr - re * ti], axis=1).astype(jnp.bfloat16)
        value = dot(value, undo_second[...])
        here = slice(s * SLAB, (s + 1) * SLAB)
        there = slice(count_one + s * SLAB, count_one + (s + 1) * SLAB)
        ur, ui = one_re[here], one_im[here]
        for n3 in range(size_c):
            lanes = slice(n3 * LANES, (n3 + 1) * LANES)
            re = value[n3 * SLAB : (n3 + 1) * SLAB, :LANES]
            im = value[n3 * SLAB : (n3 + 1) * SLAB, LANES:]
            back[here, lanes] = (re * ur + im * ui).astype(jnp.bfloat16)
            back[there, lanes] = (im * ur - re * ui).astype(jnp.bfloat16)
    result = dot(undo_first[...], back[...]).astype(jnp.bfloat16)
    for j in range(per_source):
        out_ref[0, :, j * width : (j + 1) * width] = result[j * sources : (j + 1) * sources]


def whole_block(array):
    zeros = (0,) * array.ndim
    return pl.BlockSpec(array.shape, lambda d: zeros)


def convolve(rows, filt, tables, size_c):
    channels, sources, tokens = rows.shape
    _, _, slabs, kept, _ = filt.shape
    count_one = slabs * SLAB
    return pl.pallas_call(
        functools.partial(conv_kernel, size_c),
        out_shape=jax.ShapeDtypeStruct(rows.shape, jnp.bfloat16),
        grid=(channels,),
        in_specs=[
            pl.BlockSpec((1, sources, tokens), lambda d: (d, 0, 0)),
            pl.BlockSpec((2, 1, slabs, kept, LANES), lambda d: (0, d, 0, 0, 0)),
        ]
        + [whole_block(table) for table in tables],
        out_specs=pl.BlockSpec((1, sources, tokens), lambda d: (d, 0, 0)),
        scratch_shapes=[
            pltpu.VMEM((slabs, size_c * SLAB, 2 * LANES), jnp.bfloat16),
            pltpu.VMEM((2 * count_one, B * size_c), jnp.bfloat16),
        ],
        compiler_params=pltpu.CompilerParams(vmem_limit_bytes=56 * 2**20),
        cost_estimate=pl.CostEstimate(
            flops=channels * 400_000_000, bytes_accessed=8 * 2**20, transcendentals=0
        ),
        name="spectral_conv",
    )(rows, filt, *tables)


def order_matrix(size_c):
    width = B * size_c
    col = jnp.arange(width, dtype=jnp.int32)
    origin = jnp.swapaxes(col.reshape(B, size_c), 0, 1).reshape(-1)
    return (col[:, None] == origin[None, :]).astype(jnp.bfloat16)


def short_filter(taps, which, before, block):
    extended = jnp.concatenate([before, block], axis=1).astype(jnp.float32)
    at = 3 * which
    total = taps[:, at : at + 1] * extended[:, LANES:]
    total += taps[:, at + 1 : at + 2] * pltpu.roll(extended, 1, 1)[:, LANES:]
    return total + taps[:, at + 2 : at + 3] * pltpu.roll(extended, 2, 1)[:, LANES:]


def head_kernel(halo, taps, order, ahead, block, gated_ref, sent_ref):
    first = pl.program_id(0) == 0
    filtered = [
        short_filter(taps, p, jnp.where(first, halo[p], ahead[p]), block[p]) for p in range(2)
    ]
    gated = (filtered[1] * filtered[0]).astype(jnp.bfloat16)
    gated_ref[...] = gated
    sent_ref[...] = dot(gated, order[...]).astype(jnp.bfloat16)


def head(projections, halo, taps, order):
    _, channels, tokens = projections.shape
    width = order.shape[0]
    per_block = width // LANES
    block = pl.BlockSpec((channels, width), lambda j: (0, j))
    shape = jax.ShapeDtypeStruct((channels, tokens), jnp.bfloat16)
    return pl.pallas_call(
        head_kernel,
        out_shape=(shape, shape),
        grid=(tokens // width,),
        in_specs=[
            whole_block(halo),
            whole_block(taps),
            whole_block(order),
            pl.BlockSpec(
                (2, channels, LANES), lambda j: (0, 0, jnp.maximum(j * per_block - 1, 0))
            ),
            pl.BlockSpec((2, channels, width), lambda j: (0, 0, j)),
        ],
        out_specs=(block, block),
        compiler_params=pltpu.CompilerParams(vmem_limit_bytes=56 * 2**20),
        cost_estimate=pl.CostEstimate(
            flops=2 * channels * tokens * width, bytes_accessed=16 * 2**20, transcendentals=0
        ),
        name="gate_and_reorder",
    )(halo, taps, order, projections, projections)


def tail_kernel(base, halo, taps, skip, order, ahead, block, gated, returned, out_ref):
    first = pl.program_id(0) + base == 0
    filtered = short_filter(taps, 2, jnp.where(first, halo[2], ahead[0]), block[0])
    conv = lax.dot_general(
        returned[...], order[...], (((1,), (1,)), ((), ())), preferred_element_type=jnp.float32
    )
    mix = filtered * (conv + skip[...] * gated[...].astype(jnp.float32))
    out_ref[...] = mix.astype(jnp.bfloat16)


def tail(projections, halo, taps, skip, order, gated, returned, base):
    channels, tokens = returned.shape
    width = order.shape[0]
    per_block = width // LANES
    return pl.pallas_call(
        functools.partial(tail_kernel, base),
        out_shape=jax.ShapeDtypeStruct((channels, tokens), jnp.bfloat16),
        grid=(tokens // width,),
        in_specs=[
            whole_block(halo),
            whole_block(taps),
            whole_block(skip),
            whole_block(order),
            pl.BlockSpec(
                (1, channels, LANES),
                lambda j: (2, 0, jnp.maximum((j + base) * per_block - 1, 0)),
            ),
            pl.BlockSpec((1, channels, width), lambda j: (2, 0, j + base)),
            pl.BlockSpec((channels, width), lambda j: (0, j + base)),
            pl.BlockSpec((channels, width), lambda j: (0, j)),
        ],
        out_specs=pl.BlockSpec((channels, width), lambda j: (0, j)),
        compiler_params=pltpu.CompilerParams(vmem_limit_bytes=56 * 2**20),
        cost_estimate=pl.CostEstimate(
            flops=2 * channels * tokens * width, bytes_accessed=12 * 2**20, transcendentals=0
        ),
        name="reorder_and_mix",
    )(halo, taps, skip, order, projections, projections, gated, returned)


def project(out_weight, gated_mix):
    count = lax.axis_size("chan")
    me = lax.axis_index("chan")
    depth = gated_mix.shape[0]
    held = [gated_mix] + [
        lax.ppermute(gated_mix, "chan", [(i, (i + k) % count) for i in range(count)])
        for k in range(1, count)
    ]
    total = 0.0
    for k, value in enumerate(held):
        owner = (me - k + count) % count
        weight = lax.dynamic_slice_in_dim(out_weight, owner * depth, depth, 0)
        total += jnp.einsum("de,dt->et", weight, value, preferred_element_type=jnp.float32)
    return total.astype(jnp.bfloat16)


def reordered(value, size_c, back):
    split = (size_c, B) if back else (B, size_c)
    shaped = value.reshape(value.shape[0], -1, *split)
    return jnp.swapaxes(shaped, 2, 3).reshape(value.shape)


def on_device(
    projections, short_taps, skip_gain, filter_spec, keep_first, keep_second, keep_third, out_weight
):
    tokens_here = projections.shape[2]
    ring = ("seq", "sub")
    sources = lax.axis_size(ring)
    channels = projections.shape[1] // sources
    size_c = 2 * tokens_here * sources // (A * B)
    width = B * size_c
    per_source = tokens_here // width
    count_one, count_two, count_three = (
        keep_first.shape[0],
        keep_second.shape[0],
        keep_third.shape[0],
    )
    order = order_matrix(size_c) if width <= 4096 else None

    before = passed_along(projections[:, :, tokens_here - 2 :], ring, 1)
    if order is None:
        extended = jnp.concatenate([before, projections], axis=2).astype(jnp.float32)
        filtered = (
            short_taps[:, 0, :, None] * extended[:, :, 2:]
            + short_taps[:, 1, :, None] * extended[:, :, 1:-1]
            + short_taps[:, 2, :, None] * extended[:, :, :-2]
        )
        gated_values = (filtered[1] * filtered[0]).astype(jnp.bfloat16)
        outgoing = reordered(gated_values, size_c, False)
    else:
        halo = jnp.pad(before, ((0, 0), (0, 0), (LANES - 2, 0)))
        taps = short_taps.reshape(9, -1).T
        gated_values, outgoing = head(projections, halo, taps, order)
    received = lax.all_to_all(
        outgoing.reshape(sources, channels, tokens_here), ring, split_axis=0, concat_axis=0
    )
    rows = jnp.swapaxes(received, 0, 1)

    filt = filter_spec.reshape(2, channels, count_three, count_two, count_one // SLAB, SLAB)
    filt = pad_to(jnp.transpose(filt, (0, 1, 4, 2, 5, 3)), 5, LANES)
    filt = filt.reshape(2, channels, count_one // SLAB, count_three * SLAB, LANES)
    tables = conv_tables(keep_first, keep_second, keep_third, size_c, sources, per_source)
    conv_rows = convolve(rows, filt, tables, size_c)

    conv_out = jnp.swapaxes(conv_rows, 0, 1)
    quarter = tokens_here // 4
    steps = (2 * quarter, quarter, quarter) if per_source % 4 == 0 else (tokens_here,)
    mixed = []
    ready = []
    for part, step in enumerate(steps):
        start = sum(steps[:part])
        span = slice(start, start + step)
        leaving = conv_out[:, :, span]
        if part >= 2:
            leaving, _ = lax.optimization_barrier((leaving, ready[part - 2]))
        returned = lax.all_to_all(leaving, ring, split_axis=0, concat_axis=0)
        returned = returned.reshape(sources * channels, step)
        if order is None:
            token_major = reordered(returned, size_c, True)
            gated_mix = (
                filtered[2][:, span]
                * (
                    token_major.astype(jnp.float32)
                    + skip_gain[:, None] * gated_values[:, span].astype(jnp.float32)
                )
            ).astype(jnp.bfloat16)
        else:
            gated_mix = tail(
                projections,
                halo,
                taps,
                skip_gain[:, None],
                order,
                gated_values,
                returned,
                start // width,
            )
        ready.append(gated_mix)
    mixed = [project(out_weight, gated_mix) for gated_mix in ready]
    return jnp.concatenate(mixed, axis=1)


def solution(mesh):
    placed = (
        P(None, "chan", ("groups", "seq", "sub")),
        P(None, None, "chan"),
        P("chan"),
        P(None, ("chan", "seq", "sub"), None, None),
        P(),
        P(),
        P(),
        P(None, "chan"),
    )
    return jax.shard_map(
        on_device,
        mesh=mesh,
        in_specs=placed,
        out_specs=P("chan", ("groups", "seq", "sub")),
        check_vma=False,
    )
```
